512 devices in a mesh: rep: 32 (over z, x), tp: 16 (over y, core).
Axes of the slice: x: 4, y: 8, z: 8, core: 2. Of those that a mesh axis runs over, the one named last changes fastest.
Arguments:
- queries: bfloat16 [1024, 4, 128, 576], P(('rep', 'tp')), parts along dimension 0, may hold values from -26 to 26
- latent_cache: bfloat16 [1024, 1024, 576], P(('rep', 'tp')), parts along dimension 0, may hold values from -4 to 4
- new_latent: bfloat16 [1024, 4, 576], P(('rep', 'tp')), parts along dimension 0, may hold values from -4 to 4
- cached_lengths: int32 [1024], P(('rep', 'tp')), parts along dimension 0, may hold values from 2 to 1024, as said below
- slot_rows: int32 [1024], P(('rep', 'tp')), parts along dimension 0, may hold values from 0 to 31, each once
- up_weight: bfloat16 [128, 512, 128], P('tp'), may hold values from -0.25 to 0.25
Outputs:
- attended: bfloat16 [1024, 4, 16384], P(('rep', 'tp')), parts along dimension 0
The draws below stay inside these ranges and needn't reach their ends.
There are 32 independent parts, one for each index of `rep`. The reference program is written for one: setup_inputs(seed, part) draws one part's arguments, and reference() takes and returns one part's arrays. A program takes and returns all parts, laid end to end along the dimension named above; an argument that names none is the same for every part. Nothing has to cross between parts.
Inputs may be any that keep to these rules, and one draw needn't show every extreme that they name: `cached_lengths`: some slot has exactly 1024 cached positions. `slot_rows`: each row of the group is held by exactly one slot.
All inputs are finite; a program needn't handle non-finite values.
Results may differ from the reference program's by a relative error of at most 0.0052.
Values may be sent and summed in bfloat16 or wider, within the bound.
A program may use at most 64 MiB of HBM per device.

```python
import jax
import jax.numpy as jnp
from jax import lax

H = 128
LAT = 512
ROPE = 64
NOPE = 128
VDIM = 128
STEPS = 4
CTX = 1024
ROWS = 32


def cache_values(key):
    return jnp.clip(jax.random.normal(key, (ROWS, CTX, LAT + ROPE), jnp.float32), -4.0, 4.0)


def draw_latent_cache(key, part):
    base_cache = cache_values(key)
    return base_cache.astype(jnp.bfloat16)


def draw_queries(key, part):
    key = jax.random.fold_in(key, 12)
    shape_full = (ROWS, STEPS, H, LAT + ROPE)
    drawn = jnp.clip(jax.random.normal(key, shape_full, jnp.float32), -6.0, 6.0)
    return drawn.astype(jnp.bfloat16)


def draw_cached_lengths(key, part):
    key = jax.random.fold_in(key, 13)
    first_key, second_key = jax.random.split(key)
    lengths_drawn = jax.random.randint(first_key, (ROWS,), 2, CTX + 1)
    longest = jax.random.randint(second_key, (), 0, ROWS)
    return lengths_drawn.at[longest].set(CTX).astype(jnp.int32)


def steps_of(own_key, dims, pieces, low, largest):
    level = 1.0
    for position, shards_of in pieces:
        draws = jax.random.uniform(jax.random.fold_in(jax.random.fold_in(own_key, 6), position), (shards_of,), jnp.float32, low / len(pieces), largest / len(pieces))
        level = level * jnp.repeat(jnp.exp(draws), dims[position] // shards_of).reshape((-1,) + (1,) * (len(dims) - 1 - position))
    return level


def gaussian(own_key, shape, width, most, cuts=(), held_as=jnp.bfloat16):
    level = steps_of(own_key, shape, cuts, -0.22, 0.18) if cuts else 1.0
    values = jax.random.normal(own_key, shape, jnp.float32) * width * level
    return jnp.minimum(jnp.maximum(values, -most), most).astype(held_as)


def setup_inputs(seed: int = 0, part: int = 0) -> dict:
    keys = jax.random.split(jax.random.key(seed), 7)
    part_keys = jax.random.split(jax.random.fold_in(keys[6], part), 7)
    return {
        "queries": draw_queries(jax.random.fold_in(jax.random.fold_in(keys[6], part), 71), part),
        "latent_cache": draw_latent_cache(jax.random.fold_in(jax.random.fold_in(keys[6], part), 71), part),
        "new_latent": gaussian(part_keys[2], (ROWS, STEPS, LAT + ROPE), 1.0, 4.0, ((0, 16),)),
        "cached_lengths": draw_cached_lengths(jax.random.fold_in(jax.random.fold_in(keys[6], part), 71), part),
        "slot_rows": jax.random.permutation(part_keys[4], ROWS).astype(jnp.int32),
        "up_weight": gaussian(keys[5], (H, LAT, VDIM), LAT ** -0.5, 0.25, ((0, 16),)),
    }


def attend_slot(packed):
    query_rows, slot_keys, fresh_keys, length = packed
    draft_count, head_count, embed_dim = query_rows.shape
    softmax_scale = (NOPE + ROPE) ** -0.5
    flat_queries = query_rows.reshape(draft_count * head_count, embed_dim)
    old_scores = jnp.dot(flat_queries, slot_keys.T, preferred_element_type=jnp.float32) * softmax_scale
    new_scores = jnp.dot(flat_queries, fresh_keys.T, preferred_element_type=jnp.float32) * softmax_scale
    old_valid = jnp.arange(slot_keys.shape[0])[None, :] < length
    row_step = jnp.arange(draft_count * head_count) // head_count
    new_valid = jnp.arange(draft_count)[None, :] <= row_step[:, None]
    old_scores = jnp.where(old_valid, old_scores, -jnp.inf)
    new_scores = jnp.where(new_valid, new_scores, -jnp.inf)
    row_top = jnp.maximum(jnp.max(old_scores, axis=1), jnp.max(new_scores, axis=1))
    old_exp = jnp.exp(old_scores - row_top[:, None])
    new_exp = jnp.exp(new_scores - row_top[:, None])
    row_total = jnp.sum(old_exp, axis=1) + jnp.sum(new_exp, axis=1)
    mixed_sum = jnp.dot(old_exp.astype(jnp.bfloat16), slot_keys[:, :LAT], preferred_element_type=jnp.float32)
    mixed_sum = mixed_sum + jnp.dot(new_exp.astype(jnp.bfloat16), fresh_keys[:, :LAT], preferred_element_type=jnp.float32)
    latents = (mixed_sum / row_total[:, None]).astype(jnp.bfloat16)
    return latents.reshape(draft_count, head_count, LAT)


def reference(queries, latent_cache, new_latent, cached_lengths, slot_rows, up_weight):
    latents = lax.map(attend_slot, (queries, latent_cache, new_latent, cached_lengths))
    head_values = jnp.einsum("rshl,hlv->rshv", latents.astype(jnp.float32), up_weight.astype(jnp.float32))
    head_values = head_values.astype(jnp.bfloat16).reshape(ROWS, STEPS, H * VDIM)
    attended = jnp.zeros((ROWS, STEPS, H * VDIM), jnp.bfloat16)
    return attended.at[slot_rows].set(head_values)
```

```python
import functools
import math

import jax
import jax.numpy as jnp
from jax import lax
from jax.experimental import pallas as pl
from jax.experimental.pallas import tpu as pltpu
from jax.sharding import PartitionSpec as P

ROPE = 64
NOPE = 128
MESH = pl.DeviceIdType.MESH

ORDER = (8, 9, 7, 10, 6, 11, 5, 12, 4, 13, 3, 14, 2, 15, 1, 0)
PER_GROUP = 4


def kernel(
    n,
    lengths_ref,
    rows_ref,
    q_hbm,
    cache_hbm,
    new_ref,
    up_hbm,
    out_ref,
    q_ref,
    cache_ref,
    up_ref,
    send1,
    recv1,
    send2,
    recv2,
    rows_out,
    rows_in,
    load_sem,
    rows_send_sem,
    rows_recv_sem,
    send1_sem,
    recv1_sem,
    own1_sem,
    send2_sem,
    recv2_sem,
    own2_sem,
):
    rep = lax.axis_index("rep")
    me = lax.axis_index("tp")
    slots, drafts, heads, _ = q_ref.shape
    ctx = cache_ref.shape[1]
    lat, values = up_hbm.shape[1], up_hbm.shape[2]
    own_heads = up_hbm.shape[0]
    pairs = drafts // 2
    groups = n // PER_GROUP
    per_block = slots * 2 * own_heads
    group_rows = PER_GROUP * per_block
    scale = (NOPE + ROPE) ** -0.5 * math.log2(math.e)

    barrier = pltpu.get_barrier_semaphore()
    for k in range(1, n):
        pl.semaphore_signal(barrier, inc=1, device_id=(rep, (me + k) % n), device_id_type=MESH)

    loads = []
    for b in range(slots):
        loads.append(
            (
                pltpu.make_async_copy(cache_hbm.at[b], cache_ref.at[b], load_sem.at[2 * b]),
                pltpu.make_async_copy(q_hbm.at[b], q_ref.at[b], load_sem.at[2 * b + 1]),
            )
        )
        for copy in loads[-1]:
            copy.start()
    up_loads = []
    for h in range(own_heads):
        copy = pltpu.make_async_copy(
            up_hbm.at[h], up_ref.at[:, pl.ds(h * values, values)], load_sem.at[2 * slots + h]
        )
        copy.start()
        up_loads.append(copy)

    lane = lax.broadcasted_iota(jnp.int32, (8, 128), 1)
    rows_out[...] = jnp.where((lane // (2 * own_heads)) % 2 == 0, rows_ref[0], rows_ref[1])

    def attend(b, pair):
        q = q_ref[b, pl.ds(2 * pair, 2)].reshape(2 * heads, q_ref.shape[3])
        keys = cache_ref[b]
        fresh = new_ref[b]
        contract = (((1,), (1,)), ((), ()))
        old = lax.dot_general(q, keys, contract, preferred_element_type=jnp.float32)
        new = lax.dot_general(q, fresh, contract, preferred_element_type=jnp.float32)
        position = lax.broadcasted_iota(jnp.int32, (1, ctx), 1)
        old = jnp.where(position < lengths_ref[b], old, -jnp.inf)
        step = 2 * pair + lax.broadcasted_iota(jnp.int32, new.shape, 0) // heads
        new = jnp.where(lax.broadcasted_iota(jnp.int32, new.shape, 1) <= step, new, -jnp.inf)
        top = jnp.maximum(jnp.max(old, axis=1, keepdims=True), jnp.max(new, axis=1, keepdims=True))
        old = jnp.exp2((old - top) * scale)
        new = jnp.exp2((new - top) * scale)
        total = jnp.sum(old, axis=1, keepdims=True) + jnp.sum(new, axis=1, keepdims=True)
        mixed = jnp.dot(old.astype(jnp.bfloat16), keys[:, :lat], preferred_element_type=jnp.float32)
        mixed = mixed + jnp.dot(new.astype(jnp.bfloat16), fresh[:, :lat], preferred_element_type=jnp.float32)
        latents = mixed * (1.0 / total)
        latents = latents.reshape(2, n, own_heads, lat)
        for d in range(n):
            block = jnp.concatenate([latents[0, d], latents[1, d]], axis=0)
            send1[pair, d, pl.ds(b * 2 * own_heads, 2 * own_heads), :] = block.astype(jnp.bfloat16)

    def send_first(pair):
        for p, k in enumerate(ORDER):
            to = (me + k) % n
            if k == 0:
                pltpu.make_async_copy(send1.at[pair, me], recv1.at[pair, p], own1_sem.at[pair]).start()
            else:
                pltpu.make_async_remote_copy(
                    src_ref=send1.at[pair, to],
                    dst_ref=recv1.at[pair, p],
                    send_sem=send1_sem.at[pair],
                    recv_sem=recv1_sem.at[pair, p // PER_GROUP],
                    device_id=(rep, to),
                    device_id_type=MESH,
                ).start()

    for pair in range(pairs):
        for b in range(slots):
            if pair == 0:
                for copy in loads[b]:
                    copy.wait()
            attend(b, pair)
        if pair == 0:
            pl.semaphore_wait(barrier, n - 1)
            for p, k in enumerate(ORDER):
                if k:
                    pltpu.make_async_remote_copy(
                        src_ref=rows_out,
                        dst_ref=rows_in.at[p],
                        send_sem=rows_send_sem,
                        recv_sem=rows_recv_sem,
                        device_id=(rep, (me + k) % n),
                        device_id_type=MESH,
                    ).start()
        send_first(pair)

    for copy in up_loads:
        copy.wait()
    pltpu.make_async_copy(rows_in.at[pl.ds(0, n - 1)], rows_in.at[pl.ds(0, n - 1)], rows_recv_sem).wait()
    rows_in[n - 1] = rows_out[...]

    out_lines = n * 16
    o = lax.broadcasted_iota(jnp.int32, (out_lines, group_rows), 0)
    i = lax.broadcasted_iota(jnp.int32, (out_lines, group_rows), 1)
    want = (o // 16) * 2 + (o // 2) % 2
    same_draft = (o % 2) == (i // own_heads) % 2
    source = lax.broadcasted_iota(jnp.int32, (1, group_rows), 1) // per_block
    picks = []
    for g in range(groups):
        held = rows_in[g * PER_GROUP][0:1]
        for s in range(1, PER_GROUP):
            held = jnp.where(source == s, rows_in[g * PER_GROUP + s][0:1], held)
        picks.append(jnp.where((want == held) & same_draft, 1.0, 0.0).astype(jnp.bfloat16))

    line_head = lax.broadcasted_iota(jnp.int32, (group_rows, values), 0) % own_heads
    quarter = (lax.broadcasted_iota(jnp.int32, (out_lines, 256), 0) // 4) % 4

    for pair in range(pairs):
        ordered = None
        for g in range(groups):
            first = g * PER_GROUP
            count = min(PER_GROUP, n - 1 - first)
            arrived = recv1.at[pair, pl.ds(first, count)]
            pltpu.make_async_copy(arrived, arrived, recv1_sem.at[pair, g]).wait()
            if count < PER_GROUP:
                pltpu.make_async_copy(send1.at[pair, me], recv1.at[pair, n - 1], own1_sem.at[pair]).wait()
            block = recv1[pair, pl.ds(first, PER_GROUP)].reshape(group_rows, lat)
            full = jnp.dot(block, up_ref[...], preferred_element_type=jnp.float32)
            kept = jnp.concatenate(
                [
                    jnp.where(line_head == h, full[:, h * values : (h + 1) * values], 0.0).astype(jnp.bfloat16)
                    for h in range(own_heads)
                ],
                axis=1,
            )
            part = jnp.dot(picks[g], kept, preferred_element_type=jnp.float32)
            ordered = part if ordered is None else ordered + part
        block = ordered[:, :256]
        for s in range(1, 4):
            block = jnp.where(quarter == s, ordered[:, s * 256 : (s + 1) * 256], block)
        send2[pair] = block.astype(jnp.bfloat16).reshape(n, 16, 256)
        columns = pl.ds(pl.multiple_of(me * 256, 256), 256)
        landing = recv2.at[pl.ds(pair * 16, 16), columns]
        for k in ORDER:
            to = (me + k) % n
            if k == 0:
                pltpu.make_async_copy(send2.at[pair, me], landing, own2_sem.at[pair]).start()
            else:
                pltpu.make_async_remote_copy(
                    src_ref=send2.at[pair, to],
                    dst_ref=landing,
                    send_sem=send2_sem.at[pair],
                    recv_sem=recv2_sem.at[pair],
                    device_id=(rep, to),
                    device_id_type=MESH,
                ).start()

    for pair in range(pairs):
        arrived = recv2.at[pl.ds(pair * 16, 16), pl.ds(0, (n - 1) * 256)]
        pltpu.make_async_copy(arrived, arrived, recv2_sem.at[pair]).wait()
        own = recv2.at[pl.ds(pair * 16, 16), pl.ds(pl.multiple_of(me * 256, 256), 256)]
        pltpu.make_async_copy(send2.at[pair, me], own, own2_sem.at[pair]).wait()

    lines = 4 * slots * drafts
    o = lax.broadcasted_iota(jnp.int32, (lines, pairs * 16), 0)
    i = lax.broadcasted_iota(jnp.int32, (lines, pairs * 16), 1)
    wanted = ((o % 4) // 2) * 16 + (o // 8) * 4 + ((o // 4) % 2) * 2 + o % 2
    place = jnp.where(i == wanted, 1.0, 0.0).astype(jnp.bfloat16)
    final = jnp.dot(place, recv2[...], preferred_element_type=jnp.float32)
    for s in range(n):
        for t in range(4):
            out_ref[:, pl.ds(s * 1024 + t * 256, 256)] = final[t * 8 : (t + 1) * 8, s * 256 : (s + 1) * 256].astype(
                jnp.bfloat16
            )

    pltpu.make_async_copy(rows_in.at[pl.ds(0, n - 1)], rows_in.at[pl.ds(0, n - 1)], rows_send_sem).wait()
    for pair in range(pairs):
        sent = send1.at[pair, pl.ds(0, n - 1)]
        pltpu.make_async_copy(sent, sent, send1_sem.at[pair]).wait()
        sent = send2.at[pair, pl.ds(0, n - 1)]
        pltpu.make_async_copy(sent, sent, send2_sem.at[pair]).wait()


def per_device(n, queries, latent_cache, new_latent, cached_lengths, slot_rows, up_weight):
    slots, drafts, heads, embed = queries.shape
    own_heads, lat, values = up_weight.shape
    ctx = latent_cache.shape[1]
    pairs = drafts // 2
    per_block = slots * 2 * own_heads
    smem = pl.BlockSpec(memory_space=pltpu.SMEM)
    vmem = pl.BlockSpec(memory_space=pltpu.VMEM)
    hbm = pl.BlockSpec(memory_space=pl.ANY)
    dma = pltpu.SemaphoreType.DMA
    bf16 = jnp.bfloat16
    out = pl.pallas_call(
        functools.partial(kernel, n),
        out_shape=jax.ShapeDtypeStruct((slots * drafts, heads * values), bf16),
        in_specs=[smem, smem, hbm, hbm, vmem, hbm],
        out_specs=vmem,
        scratch_shapes=[
            pltpu.VMEM((slots, drafts, heads, embed), bf16),
            pltpu.VMEM((slots, ctx, embed), bf16),
            pltpu.VMEM((lat, own_heads * values), bf16),
            pltpu.VMEM((pairs, n, per_block, lat), bf16),
            pltpu.VMEM((pairs, n, per_block, lat), bf16),
            pltpu.VMEM((pairs, n, 16, 256), bf16),
            pltpu.VMEM((pairs * 16, n * 256), bf16),
            pltpu.VMEM((8, 128), jnp.int32),
            pltpu.VMEM((n, 8, 128), jnp.int32),
            dma((2 * slots + own_heads,)),
            dma,
            dma,
            dma((pairs,)),
            dma((pairs, n // PER_GROUP)),
            dma((pairs,)),
            dma((pairs,)),
            dma((pairs,)),
            dma((pairs,)),
        ],
        compiler_params=pltpu.CompilerParams(collective_id=0, has_side_effects=True, vmem_limit_bytes=48 << 20),
    )(cached_lengths, slot_rows, queries, latent_cache, new_latent, up_weight)
    return out.reshape(slots, drafts, heads * values)


def solution(mesh):
    return jax.shard_map(
        functools.partial(per_device, mesh.shape["tp"]),
        mesh=mesh,
        in_specs=(
            P(("rep", "tp"), None, None, None),
            P(("rep", "tp"), None, None),
            P(("rep", "tp"), None, None),
            P(("rep", "tp")),
            P(("rep", "tp")),
            P("tp", None, None),
        ),
        out_specs=P(("rep", "tp"), None, None),
        check_vma=False,
    )
```

```python
import functools
import math

import jax
import jax.numpy as jnp
from jax import lax
from jax.experimental import pallas as pl
from jax.experimental.pallas import tpu as pltpu
from jax.sharding import PartitionSpec as P

ROPE = 64
NOPE = 128
MESH = pl.DeviceIdType.MESH

ORDER = (8, 9, 7, 10, 6, 11, 5, 12, 4, 13, 3, 14, 2, 15, 1, 0)
PER_GROUP = 4


def kernel(
    n,
    lengths_ref,
    rows_ref,
    q_hbm,
    cache_hbm,
    new_ref,
    up_hbm,
    out_ref,
    q_ref,
    cache_ref,
    up_ref,
    send1,
    recv1,
    send2,
    recv2,
    rows_out,
    rows_in,
    load_sem,
    rows_send_sem,
    rows_recv_sem,
    send1_sem,
    recv1_sem,
    own1_sem,
    send2_sem,
    recv2_sem,
    own2_sem,
):
    rep = lax.axis_index("rep")
    me = lax.axis_index("tp")
    slots, drafts, _, heads = q_ref.shape
    ctx = cache_ref.shape[2]
    lat, values = up_hbm.shape[1], up_hbm.shape[2]
    own_heads = up_hbm.shape[0]
    pairs = drafts // 2
    groups = n // PER_GROUP
    per_block = slots * 2 * own_heads
    group_rows = PER_GROUP * per_block
    scale = (NOPE + ROPE) ** -0.5 * math.log2(math.e)

    barrier = pltpu.get_barrier_semaphore()
    for k in range(1, n):
        pl.semaphore_signal(barrier, inc=1, device_id=(rep, (me + k) % n), device_id_type=MESH)

    loads = []
    for b in range(slots):
        loads.append(
            (
                pltpu.make_async_copy(cache_hbm.at[b], cache_ref.at[b], load_sem.at[2 * b]),
                pltpu.make_async_copy(q_hbm.at[b], q_ref.at[b], load_sem.at[2 * b + 1]),
            )
        )
        for copy in loads[-1]:
            copy.start()
    up_loads = []
    for h in range(own_heads):
        copy = pltpu.make_async_copy(
            up_hbm.at[h], up_ref.at[:, pl.ds(h * values, values)], load_sem.at[2 * slots + h]
        )
        copy.start()
        up_loads.append(copy)

    lane = lax.broadcasted_iota(jnp.int32, (8, 128), 1)
    rows_out[...] = jnp.where((lane // (2 * own_heads)) % 2 == 0, rows_ref[0], rows_ref[1])

    def attend(b, pair):
        q = jnp.concatenate([q_ref[b, 2 * pair], q_ref[b, 2 * pair + 1]], axis=1)
        keys = cache_ref[b]
        fresh = new_ref[b]
        old = lax.dot_general(q, keys, (((0,), (0,)), ((), ())), preferred_element_type=jnp.float32)
        new = lax.dot_general(q, fresh, (((0,), (1,)), ((), ())), preferred_element_type=jnp.float32)
        position = lax.broadcasted_iota(jnp.int32, (1, ctx), 1)
        old = jnp.where(position < lengths_ref[b], old, -jnp.inf)
        step = 2 * pair + lax.broadcasted_iota(jnp.int32, new.shape, 0) // heads
        new = jnp.where(lax.broadcasted_iota(jnp.int32, new.shape, 1) <= step, new, -jnp.inf)
        top = jnp.maximum(jnp.max(old, axis=1, keepdims=True), jnp.max(new, axis=1, keepdims=True))
        old = jnp.exp2((old - top) * scale)
        new = jnp.exp2((new - top) * scale)
        total = jnp.sum(old, axis=1, keepdims=True) + jnp.sum(new, axis=1, keepdims=True)
        mixed = lax.dot_general(
            old.astype(jnp.bfloat16), keys[:lat], (((1,), (1,)), ((), ())), preferred_element_type=jnp.float32
        )
        mixed = mixed + jnp.dot(new.astype(jnp.bfloat16), fresh[:, :lat], preferred_element_type=jnp.float32)
        latents = mixed * (1.0 / total)
        latents = latents.reshape(2, n, own_heads, lat)
        for d in range(n):
            block = jnp.concatenate([latents[0, d], latents[1, d]], axis=0)
            send1[pair, d, pl.ds(b * 2 * own_heads, 2 * own_heads), :] = block.astype(jnp.bfloat16)

    def send_first(pair):
        for p, k in enumerate(ORDER):
            to = (me + k) % n
            if k == 0:
                pltpu.make_async_copy(send1.at[pair, me], recv1.at[pair, p], own1_sem.at[pair]).start()
            else:
                pltpu.make_async_remote_copy(
                    src_ref=send1.at[pair, to],
                    dst_ref=recv1.at[pair, p],
                    send_sem=send1_sem.at[pair],
                    recv_sem=recv1_sem.at[pair, p // PER_GROUP],
                    device_id=(rep, to),
                    device_id_type=MESH,
                ).start()

    for pair in range(pairs):
        for b in range(slots):
            if pair == 0:
                for copy in loads[b]:
                    copy.wait()
            attend(b, pair)
        if pair == 0:
            pl.semaphore_wait(barrier, n - 1)
            for p, k in enumerate(ORDER):
                if k:
                    pltpu.make_async_remote_copy(
                        src_ref=rows_out,
                        dst_ref=rows_in.at[p],
                        send_sem=rows_send_sem,
                        recv_sem=rows_recv_sem,
                        device_id=(rep, (me + k) % n),
                        device_id_type=MESH,
                    ).start()
        send_first(pair)

    for copy in up_loads:
        copy.wait()
    pltpu.make_async_copy(rows_in.at[pl.ds(0, n - 1)], rows_in.at[pl.ds(0, n - 1)], rows_recv_sem).wait()
    rows_in[n - 1] = rows_out[...]

    out_lines = n * 16
    o = lax.broadcasted_iota(jnp.int32, (out_lines, group_rows), 0)
    i = lax.broadcasted_iota(jnp.int32, (out_lines, group_rows), 1)
    want = (o // 16) * 2 + (o // 2) % 2
    same_draft = (o % 2) == (i // own_heads) % 2
    source = lax.broadcasted_iota(jnp.int32, (1, group_rows), 1) // per_block
    picks = []
    for g in range(groups):
        held = rows_in[g * PER_GROUP][0:1]
        for s in range(1, PER_GROUP):
            held = jnp.where(source == s, rows_in[g * PER_GROUP + s][0:1], held)
        picks.append(jnp.where((want == held) & same_draft, 1.0, 0.0).astype(jnp.bfloat16))

    line_head = lax.broadcasted_iota(jnp.int32, (group_rows, values), 0) % own_heads
    quarter = (lax.broadcasted_iota(jnp.int32, (out_lines, 256), 0) // 4) % 4

    for pair in range(pairs):
        ordered = None
        for g in range(groups):
            first = g * PER_GROUP
            count = min(PER_GROUP, n - 1 - first)
            arrived = recv1.at[pair, pl.ds(first, count)]
            pltpu.make_async_copy(arrived, arrived, recv1_sem.at[pair, g]).wait()
            if count < PER_GROUP:
                pltpu.make_async_copy(send1.at[pair, me], recv1.at[pair, n - 1], own1_sem.at[pair]).wait()
            block = recv1[pair, pl.ds(first, PER_GROUP)].reshape(group_rows, lat)
            full = jnp.dot(block, up_ref[...], preferred_element_type=jnp.float32)
            kept = jnp.concatenate(
                [
                    jnp.where(line_head == h, full[:, h * values : (h + 1) * values], 0.0).astype(jnp.bfloat16)
                    for h in range(own_heads)
                ],
                axis=1,
            )
            part = jnp.dot(picks[g], kept, preferred_element_type=jnp.float32)
            ordered = part if ordered is None else ordered + part
        block = ordered[:, :256]
        for s in range(1, 4):
            block = jnp.where(quarter == s, ordered[:, s * 256 : (s + 1) * 256], block)
        send2[pair] = block.astype(jnp.bfloat16).reshape(n, 16, 256)
        columns = pl.ds(pl.multiple_of(me * 256, 256), 256)
        landing = recv2.at[pl.ds(pair * 16, 16), columns]
        for k in ORDER:
            to = (me + k) % n
            if k == 0:
                pltpu.make_async_copy(send2.at[pair, me], landing, own2_sem.at[pair]).start()
            else:
                pltpu.make_async_remote_copy(
                    src_ref=send2.at[pair, to],
                    dst_ref=landing,
                    send_sem=send2_sem.at[pair],
                    recv_sem=recv2_sem.at[pair],
                    device_id=(rep, to),
                    device_id_type=MESH,
                ).start()

    for pair in range(pairs):
        arrived = recv2.at[pl.ds(pair * 16, 16), pl.ds(0, (n - 1) * 256)]
        pltpu.make_async_copy(arrived, arrived, recv2_sem.at[pair]).wait()
        own = recv2.at[pl.ds(pair * 16, 16), pl.ds(pl.multiple_of(me * 256, 256), 256)]
        pltpu.make_async_copy(send2.at[pair, me], own, own2_sem.at[pair]).wait()

    lines = 4 * slots * drafts
    o = lax.broadcasted_iota(jnp.int32, (lines, pairs * 16), 0)
    i = lax.broadcasted_iota(jnp.int32, (lines, pairs * 16), 1)
    wanted = ((o % 4) // 2) * 16 + (o // 8) * 4 + ((o // 4) % 2) * 2 + o % 2
    place = jnp.where(i == wanted, 1.0, 0.0).astype(jnp.bfloat16)
    final = jnp.dot(place, recv2[...], preferred_element_type=jnp.float32)
    for s in range(n):
        for t in range(4):
            out_ref[:, pl.ds(s * 1024 + t * 256, 256)] = final[t * 8 : (t + 1) * 8, s * 256 : (s + 1) * 256].astype(
                jnp.bfloat16
            )

    pltpu.make_async_copy(rows_in.at[pl.ds(0, n - 1)], rows_in.at[pl.ds(0, n - 1)], rows_send_sem).wait()
    for pair in range(pairs):
        sent = send1.at[pair, pl.ds(0, n - 1)]
        pltpu.make_async_copy(sent, sent, send1_sem.at[pair]).wait()
        sent = send2.at[pair, pl.ds(0, n - 1)]
        pltpu.make_async_copy(sent, sent, send2_sem.at[pair]).wait()


def per_device(n, queries, latent_cache, new_latent, cached_lengths, slot_rows, up_weight):
    slots, drafts, heads, embed = queries.shape
    own_heads, lat, values = up_weight.shape
    ctx = latent_cache.shape[1]
    pairs = drafts // 2
    per_block = slots * 2 * own_heads
    smem = pl.BlockSpec(memory_space=pltpu.SMEM)
    vmem = pl.BlockSpec(memory_space=pltpu.VMEM)
    hbm = pl.BlockSpec(memory_space=pl.ANY)
    dma = pltpu.SemaphoreType.DMA
    bf16 = jnp.bfloat16
    out = pl.pallas_call(
        functools.partial(kernel, n),
        out_shape=jax.ShapeDtypeStruct((slots * drafts, heads * values), bf16),
        in_specs=[smem, smem, hbm, hbm, vmem, hbm],
        out_specs=vmem,
        scratch_shapes=[
            pltpu.VMEM((slots, drafts, embed, heads), bf16),
            pltpu.VMEM((slots, embed, ctx), bf16),
            pltpu.VMEM((lat, own_heads * values), bf16),
            pltpu.VMEM((pairs, n, per_block, lat), bf16),
            pltpu.VMEM((pairs, n, per_block, lat), bf16),
            pltpu.VMEM((pairs, n, 16, 256), bf16),
            pltpu.VMEM((pairs * 16, n * 256), bf16),
            pltpu.VMEM((8, 128), jnp.int32),
            pltpu.VMEM((n, 8, 128), jnp.int32),
            dma((2 * slots + own_heads,)),
            dma,
            dma,
            dma((pairs,)),
            dma((pairs, n // PER_GROUP)),
            dma((pairs,)),
            dma((pairs,)),
            dma((pairs,)),
            dma((pairs,)),
        ],
        compiler_params=pltpu.CompilerParams(collective_id=0, has_side_effects=True, vmem_limit_bytes=60 << 20),
    )(cached_lengths, slot_rows, queries.swapaxes(2, 3), latent_cache.swapaxes(1, 2), new_latent, up_weight)
    return out.reshape(slots, drafts, heads * values)


def solution(mesh):
    return jax.shard_map(
        functools.partial(per_device, mesh.shape["tp"]),
        mesh=mesh,
        in_specs=(
            P(("rep", "tp"), None, None, None),
            P(("rep", "tp"), None, None),
            P(("rep", "tp"), None, None),
            P(("rep", "tp")),
            P(("rep", "tp")),
            P("tp", None, None),
        ),
        out_specs=P(("rep", "tp"), None, None),
        check_vma=False,
    )
```

```python
import functools
import math

import jax
import jax.numpy as jnp
from jax import lax
from jax.experimental import pallas as pl
from jax.experimental.pallas import tpu as pltpu
from jax.sharding import PartitionSpec as P

ROPE = 64
NOPE = 128
MESH = pl.DeviceIdType.MESH

ORDER = (8, 9, 7, 10, 6, 11, 5, 12, 4, 13, 3, 14, 2, 15, 1, 0)
PER_GROUP = 4


def kernel(
    n,
    lengths_ref,
    rows_ref,
    q_hbm,
    cache_hbm,
    new_ref,
    up_hbm,
    out_ref,
    q_ref,
    cache_ref,
    up_ref,
    send1,
    recv1,
    send2,
    recv2,
    rows_out,
    rows_in,
    load_sem,
    rows_send_sem,
    rows_recv_sem,
    send1_sem,
    recv1_sem,
    own1_sem,
    send2_sem,
    recv2_sem,
    own2_sem,
    ready_sem,
):
    rep = lax.axis_index("rep")
    me = lax.axis_index("tp")
    slots, drafts, _, heads = q_ref.shape
    ctx = cache_ref.shape[2]
    lat, values = up_hbm.shape[1], up_hbm.shape[2]
    own_heads = up_hbm.shape[0]
    pairs = drafts // 2
    groups = n // PER_GROUP
    per_block = slots * 2 * own_heads
    group_rows = PER_GROUP * per_block
    scale = (NOPE + ROPE) ** -0.5 * math.log2(math.e)

    core = me % 2
    barrier = pltpu.get_barrier_semaphore()

    def announce(semaphore, offsets):
        for k in offsets:
            pl.semaphore_signal(semaphore, inc=1, device_id=(rep, (me + k) % n), device_id_type=MESH)

    announce(barrier, range(2, n, 2))

    @pl.when(core == 1)
    def _():
        announce(barrier, range(1, n, 2))

    loads = []
    for b in range(slots):
        loads.append(
            (
                pltpu.make_async_copy(cache_hbm.at[b], cache_ref.at[b], load_sem.at[2 * b]),
                pltpu.make_async_copy(q_hbm.at[b], q_ref.at[b], load_sem.at[2 * b + 1]),
            )
        )
        for copy in loads[-1]:
            copy.start()
    up_loads = []
    for h in range(own_heads):
        copy = pltpu.make_async_copy(
            up_hbm.at[h], up_ref.at[:, pl.ds(h * values, values)], load_sem.at[2 * slots + h]
        )
        copy.start()
        up_loads.append(copy)

    chunks = lat // 128
    lines_slot = 2 * own_heads
    per_slot = lines_slot * chunks
    lane = lax.broadcasted_iota(jnp.int32, (1, 128), 1)
    rows_out[...] = jnp.where((lane // lines_slot) % 2 == 0, rows_ref[0], rows_ref[1])

    def attend(b, pair):
        q = jnp.concatenate([q_ref[b, 2 * pair], q_ref[b, 2 * pair + 1]], axis=1)
        keys = cache_ref[b]
        fresh = new_ref[b]
        old = lax.dot_general(q, keys, (((0,), (0,)), ((), ())), preferred_element_type=jnp.float32)
        new = lax.dot_general(q, fresh, (((0,), (1,)), ((), ())), preferred_element_type=jnp.float32)
        position = lax.broadcasted_iota(jnp.int32, (1, ctx), 1)
        old = jnp.where(position < lengths_ref[b], old, -jnp.inf)
        step = 2 * pair + lax.broadcasted_iota(jnp.int32, new.shape, 0) // heads
        new = jnp.where(lax.broadcasted_iota(jnp.int32, new.shape, 1) <= step, new, -jnp.inf)
        top = jnp.maximum(jnp.max(old, axis=1, keepdims=True), jnp.max(new, axis=1, keepdims=True))
        old = jnp.exp2((old - top) * scale)
        new = jnp.exp2((new - top) * scale)
        total = jnp.sum(old, axis=1, keepdims=True) + jnp.sum(new, axis=1, keepdims=True)
        mixed = lax.dot_general(
            old.astype(jnp.bfloat16), keys[:lat], (((1,), (1,)), ((), ())), preferred_element_type=jnp.float32
        )
        mixed = mixed + jnp.dot(new.astype(jnp.bfloat16), fresh[:, :lat], preferred_element_type=jnp.float32)
        latents = mixed * (1.0 / total)
        latents = latents.reshape(2, n, own_heads, lat)
        for d in range(n):
            block = jnp.concatenate([latents[0, d], latents[1, d]], axis=0).astype(jnp.bfloat16)
            for c in range(chunks):
                send1[pair, d, pl.ds(b * per_slot + c * lines_slot, lines_slot), :] = block[:, c * 128 : (c + 1) * 128]

    def send_first(pair, odd, first, last):
        part = pl.ds(first, last - first)
        for p, k in enumerate(ORDER):
            to = (me + k) % n
            if k % 2 != odd:
                continue
            if k == 0:
                if last == slots * per_slot:
                    pltpu.make_async_copy(send1.at[pair, me], recv1.at[pair, p], own1_sem.at[pair]).start()
                continue
            pltpu.make_async_remote_copy(
                src_ref=send1.at[pair, to, part],
                dst_ref=recv1.at[pair, p, part],
                send_sem=send1_sem.at[pair],
                recv_sem=recv1_sem.at[pair, p // PER_GROUP],
                device_id=(rep, to),
                device_id_type=MESH,
            ).start()

    def send_rows(odd):
        for p, k in enumerate(ORDER):
            if k and k % 2 == odd:
                pltpu.make_async_remote_copy(
                    src_ref=rows_out,
                    dst_ref=rows_in.at[p],
                    send_sem=rows_send_sem,
                    recv_sem=rows_recv_sem,
                    device_id=(rep, (me + k) % n),
                    device_id_type=MESH,
                ).start()

    for pair in range(pairs):
        for b in range(slots):
            if pair == 0:
                for copy in loads[b]:
                    copy.wait()
            attend(b, pair)
            if pair == 0 and b == 0:
                pl.semaphore_wait(barrier, n // 2 - 1 + (n // 2) * (1 - core))

                @pl.when(core == 0)
                def _():
                    announce(ready_sem, range(1, n, 2))

            if pair == 0:
                first, last = b * per_slot, (b + 1) * per_slot
            elif b == slots - 1:
                first, last = 0, slots * per_slot
            else:
                continue
            send_first(pair, 0, first, last)

            @pl.when(core == 0)
            def _():
                send_first(pair, 1, first, last)

            if pair == 0 and b == 0:
                send_rows(0)

                @pl.when(core == 0)
                def _():
                    send_rows(1)

    @pl.when(core == 1)
    def _():
        pl.semaphore_wait(ready_sem, n // 2)
        for pair in range(pairs):
            send_first(pair, 1, 0, slots * per_slot)
            if pair == 0:
                send_rows(1)

    for copy in up_loads:
        copy.wait()

    out_lines = n * 16
    o = lax.broadcasted_iota(jnp.int32, (out_lines, group_rows), 0)
    i = lax.broadcasted_iota(jnp.int32, (out_lines, group_rows), 1)
    want = (o // 16) * 2 + (o // 2) % 2
    same_draft = (o % 2) == (i // own_heads) % 2
    source = lax.broadcasted_iota(jnp.int32, (1, group_rows), 1) // per_block
    picks = []
    pltpu.make_async_copy(rows_in.at[pl.ds(0, n - 1)], rows_in.at[pl.ds(0, n - 1)], rows_recv_sem).wait()
    rows_in[n - 1] = rows_out[...]

    def pick(g):
        held = rows_in[g * PER_GROUP]
        for s in range(1, PER_GROUP):
            held = jnp.where(source == s, rows_in[g * PER_GROUP + s], held)
        return jnp.where((want == held) & same_draft, 1.0, 0.0).astype(jnp.bfloat16)

    line_head = lax.broadcasted_iota(jnp.int32, (group_rows, values), 0) % own_heads
    quarter = (lax.broadcasted_iota(jnp.int32, (out_lines, 256), 0) // 4) % 4

    for pair in range(pairs):
        ordered = None
        for g in range(groups):
            first = g * PER_GROUP
            count = min(PER_GROUP, n - 1 - first)
            arrived = recv1.at[pair, pl.ds(first, count)]
            pltpu.make_async_copy(arrived, arrived, recv1_sem.at[pair, g]).wait()
            if count < PER_GROUP:
                pltpu.make_async_copy(send1.at[pair, me], recv1.at[pair, n - 1], own1_sem.at[pair]).wait()
            if pair == 0:
                picks.append(pick(g))
            block = recv1[pair, pl.ds(first, PER_GROUP)]
            block = block.reshape(PER_GROUP * slots, chunks, lines_slot, 128)
            block = jnp.concatenate([block[:, c] for c in range(chunks)], axis=2).reshape(group_rows, lat)
            full = jnp.dot(block, up_ref[...], preferred_element_type=jnp.float32)
            kept = jnp.concatenate(
                [
                    jnp.where(line_head == h, full[:, h * values : (h + 1) * values], 0.0).astype(jnp.bfloat16)
                    for h in range(own_heads)
                ],
                axis=1,
            )
            part = jnp.dot(picks[g], kept, preferred_element_type=jnp.float32)
            ordered = part if ordered is None else ordered + part
        block = ordered[:, :256]
        for s in range(1, 4):
            block = jnp.where(quarter == s, ordered[:, s * 256 : (s + 1) * 256], block)
        send2[pair] = block.astype(jnp.bfloat16).reshape(n, 16, 256)
        columns = pl.ds(pl.multiple_of(me * 256, 256), 256)
        landing = recv2.at[pl.ds(pair * 16, 16), columns]
        for k in ORDER:
            to = (me + k) % n
            if k == 0:
                pltpu.make_async_copy(send2.at[pair, me], landing, own2_sem.at[pair]).start()
            else:
                pltpu.make_async_remote_copy(
                    src_ref=send2.at[pair, to],
                    dst_ref=landing,
                    send_sem=send2_sem.at[pair],
                    recv_sem=recv2_sem.at[pair],
                    device_id=(rep, to),
                    device_id_type=MESH,
                ).start()

    for pair in range(pairs):
        arrived = recv2.at[pl.ds(pair * 16, 16), pl.ds(0, (n - 1) * 256)]
        pltpu.make_async_copy(arrived, arrived, recv2_sem.at[pair]).wait()
        own = recv2.at[pl.ds(pair * 16, 16), pl.ds(pl.multiple_of(me * 256, 256), 256)]
        pltpu.make_async_copy(send2.at[pair, me], own, own2_sem.at[pair]).wait()

    lines = 4 * slots * drafts
    o = lax.broadcasted_iota(jnp.int32, (lines, pairs * 16), 0)
    i = lax.broadcasted_iota(jnp.int32, (lines, pairs * 16), 1)
    wanted = ((o % 4) // 2) * 16 + (o // 8) * 4 + ((o // 4) % 2) * 2 + o % 2
    place = jnp.where(i == wanted, 1.0, 0.0).astype(jnp.bfloat16)
    final = jnp.dot(place, recv2[...], preferred_element_type=jnp.float32)
    for s in range(n):
        for t in range(4):
            lines = final[t * 8 : (t + 1) * 8, s * 256 : (s + 1) * 256].astype(jnp.bfloat16)
            out_ref[:, :, pl.ds(s * 1024 + t * 256, 256)] = lines.reshape(slots, drafts, 256)

    pltpu.make_async_copy(rows_in.at[pl.ds(0, n - 1)], rows_in.at[pl.ds(0, n - 1)], rows_send_sem).wait()
    for pair in range(pairs):
        sent = send1.at[pair, pl.ds(0, n - 1)]
        pltpu.make_async_copy(sent, sent, send1_sem.at[pair]).wait()
        sent = send2.at[pair, pl.ds(0, n - 1)]
        pltpu.make_async_copy(sent, sent, send2_sem.at[pair]).wait()


def per_device(n, queries, latent_cache, new_latent, cached_lengths, slot_rows, up_weight):
    slots, drafts, heads, embed = queries.shape
    own_heads, lat, values = up_weight.shape
    ctx = latent_cache.shape[1]
    pairs = drafts // 2
    per_block = slots * 2 * own_heads
    smem = pl.BlockSpec(memory_space=pltpu.SMEM)
    vmem = pl.BlockSpec(memory_space=pltpu.VMEM)
    hbm = pl.BlockSpec(memory_space=pl.ANY)
    dma = pltpu.SemaphoreType.DMA
    bf16 = jnp.bfloat16
    return pl.pallas_call(
        functools.partial(kernel, n),
        out_shape=jax.ShapeDtypeStruct((slots, drafts, heads * values), bf16),
        in_specs=[smem, smem, hbm, hbm, vmem, hbm],
        out_specs=vmem,
        scratch_shapes=[
            pltpu.VMEM((slots, drafts, embed, heads), bf16),
            pltpu.VMEM((slots, embed, ctx), bf16),
            pltpu.VMEM((lat, own_heads * values), bf16),
            pltpu.VMEM((pairs, n, per_block * lat // 128, 128), bf16),
            pltpu.VMEM((pairs, n, per_block * lat // 128, 128), bf16),
            pltpu.VMEM((pairs, n, 16, 256), bf16),
            pltpu.VMEM((pairs * 16, n * 256), bf16),
            pltpu.VMEM((1, 128), jnp.int32),
            pltpu.VMEM((n, 1, 128), jnp.int32),
            dma((2 * slots + own_heads,)),
            dma,
            dma,
            dma((pairs,)),
            dma((pairs, n // PER_GROUP)),
            dma((pairs,)),
            dma((pairs,)),
            dma((pairs,)),
            dma((pairs,)),
            pltpu.SemaphoreType.REGULAR,
        ],
        compiler_params=pltpu.CompilerParams(collective_id=0, has_side_effects=True, vmem_limit_bytes=60 << 20),
    )(cached_lengths, slot_rows, queries.swapaxes(2, 3), latent_cache.swapaxes(1, 2), new_latent, up_weight)


def solution(mesh):
    return jax.shard_map(
        functools.partial(per_device, mesh.shape["tp"]),
        mesh=mesh,
        in_specs=(
            P(("rep", "tp"), None, None, None),
            P(("rep", "tp"), None, None),
            P(("rep", "tp"), None, None),
            P(("rep", "tp")),
            P(("rep", "tp")),
            P("tp", None, None),
        ),
        out_specs=P(("rep", "tp"), None, None),
        check_vma=False,
    )
```

```python
import functools
import math

import jax
import jax.numpy as jnp
from jax import lax
from jax.experimental import pallas as pl
from jax.experimental.pallas import tpu as pltpu
from jax.sharding import PartitionSpec as P

ROPE = 64
NOPE = 128
MESH = pl.DeviceIdType.MESH

ORDER = (8, 9, 7, 10, 6, 11, 5, 12, 4, 13, 3, 14, 2, 15, 1, 0)
PER_GROUP = 4
EARLY = (1, 0, 2, 3)
EARLY_PAIRS = (1,)


def kernel(
    n,
    lengths_hbm,
    rows_hbm,
    q_hbm,
    cache_hbm,
    new_hbm,
    up_hbm,
    out_ref,
    lengths_ref,
    rows_ref,
    new_ref,
    q_ref,
    cache_ref,
    up_ref,
    send1,
    recv1,
    send2,
    recv2,
    rows_out,
    rows_in,
    small_sem,
    load_sem,
    rows_send_sem,
    rows_recv_sem,
    send1_sem,
    recv1_sem,
    own1_sem,
    send2_sem,
    recv2_sem,
    own2_sem,
    ready_sem,
):
    rep = lax.axis_index("rep")
    me = lax.axis_index("tp")
    slots, drafts, _, heads = q_ref.shape
    ctx = cache_ref.shape[2]
    lat, values = up_hbm.shape[1], up_hbm.shape[2]
    own_heads = up_hbm.shape[0]
    pairs = drafts // 2
    groups = n // PER_GROUP
    per_block = slots * 2 * own_heads
    group_rows = PER_GROUP * per_block
    scale = (NOPE + ROPE) ** -0.5 * math.log2(math.e)

    core = me % 2
    barrier = pltpu.get_barrier_semaphore()

    def announce(semaphore, offsets):
        for k in offsets:
            pl.semaphore_signal(semaphore, inc=1, device_id=(rep, (me + k) % n), device_id_type=MESH)

    announce(barrier, range(2, n, 2))

    @pl.when(core == 1)
    def _():
        announce(barrier, range(1, n, 2))

    small = []
    for i, (src, dst) in enumerate(((lengths_hbm, lengths_ref), (new_hbm, new_ref), (rows_hbm, rows_ref))):
        small.append(pltpu.make_async_copy(src, dst, small_sem.at[i]))
        small[-1].start()
    loads = []
    for b in range(slots):
        loads.append(
            (
                pltpu.make_async_copy(cache_hbm.at[b], cache_ref.at[b], load_sem.at[2 * b]),
                pltpu.make_async_copy(q_hbm.at[b], q_ref.at[b], load_sem.at[2 * b + 1]),
            )
        )
        if b == 0:
            for copy in loads[-1]:
                copy.start()
    up_loads = []
    for h in range(own_heads):
        copy = pltpu.make_async_copy(
            up_hbm.at[h], up_ref.at[:, pl.ds(h * values, values)], load_sem.at[2 * slots + h]
        )
        up_loads.append(copy)

    chunks = lat // 128
    lines_slot = 2 * own_heads
    per_slot = lines_slot * chunks
    lane = lax.broadcasted_iota(jnp.int32, (1, 128), 1)
    for copy in small:
        copy.wait()
    rows_out[...] = jnp.where((lane // lines_slot) % 2 == 0, rows_ref[0], rows_ref[1])

    def attend(b, pair):
        q = jnp.concatenate([q_ref[b, 2 * pair], q_ref[b, 2 * pair + 1]], axis=1)
        keys = cache_ref[b]
        fresh = new_ref[b]
        old = lax.dot_general(q, keys, (((0,), (0,)), ((), ())), preferred_element_type=jnp.float32)
        new = lax.dot_general(q, fresh, (((0,), (1,)), ((), ())), preferred_element_type=jnp.float32)
        position = lax.broadcasted_iota(jnp.int32, (1, ctx), 1)
        old = jnp.where(position < lengths_ref[b], old, -jnp.inf)
        step = 2 * pair + lax.broadcasted_iota(jnp.int32, new.shape, 0) // heads
        new = jnp.where(lax.broadcasted_iota(jnp.int32, new.shape, 1) <= step, new, -jnp.inf)
        top = jnp.maximum(jnp.max(old, axis=1, keepdims=True), jnp.max(new, axis=1, keepdims=True))
        old = jnp.exp2((old - top) * scale)
        new = jnp.exp2((new - top) * scale)
        total = jnp.sum(old, axis=1, keepdims=True) + jnp.sum(new, axis=1, keepdims=True)
        mixed = lax.dot_general(
            old.astype(jnp.bfloat16), keys[:lat], (((1,), (1,)), ((), ())), preferred_element_type=jnp.float32
        )
        mixed = mixed + jnp.dot(new.astype(jnp.bfloat16), fresh[:, :lat], preferred_element_type=jnp.float32)
        latents = mixed * (1.0 / total)
        latents = latents.reshape(2, n, own_heads, lat)
        for d in range(n):
            block = jnp.concatenate([latents[0, d], latents[1, d]], axis=0).astype(jnp.bfloat16)
            for c in range(chunks):
                send1[pair, d, pl.ds(b * per_slot + c * lines_slot, lines_slot), :] = block[:, c * 128 : (c + 1) * 128]

    def send_first(pair, odd, first, last):
        part = pl.ds(first, last - first)
        for p, k in enumerate(ORDER):
            to = (me + k) % n
            if k % 2 != odd:
                continue
            if k == 0:
                if last == slots * per_slot:
                    pltpu.make_async_copy(send1.at[pair, me], recv1.at[pair, p], own1_sem.at[pair]).start()
                continue
            pltpu.make_async_remote_copy(
                src_ref=send1.at[pair, to, part],
                dst_ref=recv1.at[pair, p, part],
                send_sem=send1_sem.at[pair],
                recv_sem=recv1_sem.at[pair, p // PER_GROUP],
                device_id=(rep, to),
                device_id_type=MESH,
            ).start()

    def send_rows(odd):
        for p, k in enumerate(ORDER):
            if k and k % 2 == odd:
                pltpu.make_async_remote_copy(
                    src_ref=rows_out,
                    dst_ref=rows_in.at[p],
                    send_sem=rows_send_sem,
                    recv_sem=rows_recv_sem,
                    device_id=(rep, (me + k) % n),
                    device_id_type=MESH,
                ).start()

    for pair in range(pairs):
        for b in range(slots):
            if pair == 0:
                for copy in loads[b]:
                    copy.wait()
                if b == 0:
                    for copy in [*loads[1], *up_loads]:
                        copy.start()
            attend(b, pair)
            if pair == 0 and b == 0:
                pl.semaphore_wait(barrier, n // 2 - 1 + (n // 2) * (1 - core))

                @pl.when(core == 0)
                def _():
                    announce(ready_sem, range(1, n, 2))

            if pair == 0:
                first, last = b * per_slot, (b + 1) * per_slot
            elif b == slots - 1:
                first, last = 0, slots * per_slot
            else:
                continue
            send_first(pair, 0, first, last)

            @pl.when(core == 0)
            def _():
                send_first(pair, 1, first, last)

            if pair == 0 and b == 0:
                send_rows(0)

                @pl.when(core == 0)
                def _():
                    send_rows(1)

    @pl.when(core == 1)
    def _():
        pl.semaphore_wait(ready_sem, n // 2)
        for pair in range(pairs):
            send_first(pair, 1, 0, slots * per_slot)
            if pair == 0:
                send_rows(1)

    for copy in up_loads:
        copy.wait()

    out_lines = n * 16
    o = lax.broadcasted_iota(jnp.int32, (out_lines, group_rows), 0)
    i = lax.broadcasted_iota(jnp.int32, (out_lines, group_rows), 1)
    want = (o // 16) * 2 + (o // 2) % 2
    same_draft = (o % 2) == (i // own_heads) % 2
    source = lax.broadcasted_iota(jnp.int32, (1, group_rows), 1) // per_block
    picks = []
    pltpu.make_async_copy(rows_in.at[pl.ds(0, n - 1)], rows_in.at[pl.ds(0, n - 1)], rows_recv_sem).wait()
    rows_in[n - 1] = rows_out[...]

    def pick(g):
        held = rows_in[g * PER_GROUP]
        for s in range(1, PER_GROUP):
            held = jnp.where(source == s, rows_in[g * PER_GROUP + s], held)
        return jnp.where((want == held) & same_draft, 1.0, 0.0).astype(jnp.bfloat16)

    line_head = lax.broadcasted_iota(jnp.int32, (group_rows, values), 0) % own_heads
    quarter = (lax.broadcasted_iota(jnp.int32, (out_lines, 256), 0) // 4) % 4

    for pair in range(pairs):
        ordered = None
        for g in range(groups):
            first = g * PER_GROUP
            count = min(PER_GROUP, n - 1 - first)
            arrived = recv1.at[pair, pl.ds(first, count)]
            pltpu.make_async_copy(arrived, arrived, recv1_sem.at[pair, g]).wait()
            if count < PER_GROUP:
                pltpu.make_async_copy(send1.at[pair, me], recv1.at[pair, n - 1], own1_sem.at[pair]).wait()
            if pair == 0:
                picks.append(pick(g))
            block = recv1[pair, pl.ds(first, PER_GROUP)]
            block = block.reshape(PER_GROUP * slots, chunks, lines_slot, 128)
            block = jnp.concatenate([block[:, c] for c in range(chunks)], axis=2).reshape(group_rows, lat)
            full = jnp.dot(block, up_ref[...], preferred_element_type=jnp.float32)
            kept = jnp.concatenate(
                [
                    jnp.where(line_head == h, full[:, h * values : (h + 1) * values], 0.0).astype(jnp.bfloat16)
                    for h in range(own_heads)
                ],
                axis=1,
            )
            part = jnp.dot(picks[g], kept, preferred_element_type=jnp.float32)
            ordered = part if ordered is None else ordered + part
        block = ordered[:, :256]
        for s in range(1, 4):
            block = jnp.where(quarter == s, ordered[:, s * 256 : (s + 1) * 256], block)
        send2[pair] = block.astype(jnp.bfloat16).reshape(n, 16, 256)
        columns = pl.ds(pl.multiple_of(me * 256, 256), 256)
        landing = recv2.at[pl.ds(pair * 16, 16), columns]
        pltpu.make_async_copy(send2.at[pair, me], landing, own2_sem.at[pair]).start()

        def send_second(to):
            pltpu.make_async_remote_copy(
                src_ref=send2.at[pair, to],
                dst_ref=landing,
                send_sem=send2_sem.at[pair],
                recv_sem=recv2_sem.at[pair],
                device_id=(rep, to),
                device_id_type=MESH,
            ).start()

        ahead = EARLY if pair in EARLY_PAIRS else ()
        for to in ahead:
            pl.when(me != to)(functools.partial(send_second, to))
        for k in ORDER[:-1]:
            to = (me + k) % n
            if ahead:
                pl.when(to >= len(ahead))(functools.partial(send_second, to))
            else:
                send_second(to)

    for pair in range(pairs):
        arrived = recv2.at[pl.ds(pair * 16, 16), pl.ds(0, (n - 1) * 256)]
        pltpu.make_async_copy(arrived, arrived, recv2_sem.at[pair]).wait()
        own = recv2.at[pl.ds(pair * 16, 16), pl.ds(pl.multiple_of(me * 256, 256), 256)]
        pltpu.make_async_copy(send2.at[pair, me], own, own2_sem.at[pair]).wait()

    lines = 4 * slots * drafts
    o = lax.broadcasted_iota(jnp.int32, (lines, pairs * 16), 0)
    i = lax.broadcasted_iota(jnp.int32, (lines, pairs * 16), 1)
    wanted = ((o % 4) // 2) * 16 + (o // 8) * 4 + ((o // 4) % 2) * 2 + o % 2
    place = jnp.where(i == wanted, 1.0, 0.0).astype(jnp.bfloat16)
    final = jnp.dot(place, recv2[...], preferred_element_type=jnp.float32)
    for s in range(n):
        for t in range(4):
            lines = final[t * 8 : (t + 1) * 8, s * 256 : (s + 1) * 256].astype(jnp.bfloat16)
            out_ref[:, :, pl.ds(s * 1024 + t * 256, 256)] = lines.reshape(slots, drafts, 256)

    pltpu.make_async_copy(rows_in.at[pl.ds(0, n - 1)], rows_in.at[pl.ds(0, n - 1)], rows_send_sem).wait()
    for pair in range(pairs):
        sent = send1.at[pair, pl.ds(0, n - 1)]
        pltpu.make_async_copy(sent, sent, send1_sem.at[pair]).wait()
        sent = send2.at[pair, pl.ds(0, n - 1)]
        pltpu.make_async_copy(sent, sent, send2_sem.at[pair]).wait()


def per_device(n, queries, latent_cache, new_latent, cached_lengths, slot_rows, up_weight):
    slots, drafts, heads, embed = queries.shape
    own_heads, lat, values = up_weight.shape
    ctx = latent_cache.shape[1]
    pairs = drafts // 2
    per_block = slots * 2 * own_heads
    vmem = pl.BlockSpec(memory_space=pltpu.VMEM)
    hbm = pl.BlockSpec(memory_space=pl.ANY)
    dma = pltpu.SemaphoreType.DMA
    bf16 = jnp.bfloat16
    return pl.pallas_call(
        functools.partial(kernel, n),
        out_shape=pltpu.VMEM((slots, drafts, heads * values), bf16),
        in_specs=[hbm] * 6,
        out_specs=vmem,
        scratch_shapes=[
            pltpu.SMEM((slots,), jnp.int32),
            pltpu.SMEM((slots,), jnp.int32),
            pltpu.VMEM((slots, drafts, embed), bf16),
            pltpu.VMEM((slots, drafts, embed, heads), bf16),
            pltpu.VMEM((slots, embed, ctx), bf16),
            pltpu.VMEM((lat, own_heads * values), bf16),
            pltpu.VMEM((pairs, n, per_block * lat // 128, 128), bf16),
            pltpu.VMEM((pairs, n, per_block * lat // 128, 128), bf16),
            pltpu.VMEM((pairs, n, 16, 256), bf16),
            pltpu.VMEM((pairs * 16, n * 256), bf16),
            pltpu.VMEM((1, 128), jnp.int32),
            pltpu.VMEM((n, 1, 128), jnp.int32),
            dma((3,)),
            dma((2 * slots + own_heads,)),
            dma,
            dma,
            dma((pairs,)),
            dma((pairs, n // PER_GROUP)),
            dma((pairs,)),
            dma((pairs,)),
            dma((pairs,)),
            dma((pairs,)),
            pltpu.SemaphoreType.REGULAR,
        ],
        compiler_params=pltpu.CompilerParams(collective_id=0, has_side_effects=True, vmem_limit_bytes=60 << 20),
    )(cached_lengths, slot_rows, queries.swapaxes(2, 3), latent_cache.swapaxes(1, 2), new_latent, up_weight)


def solution(mesh):
    return jax.shard_map(
        functools.partial(per_device, mesh.shape["tp"]),
        mesh=mesh,
        in_specs=(
            P(("rep", "tp"), None, None, None),
            P(("rep", "tp"), None, None),
            P(("rep", "tp"), None, None),
            P(("rep", "tp")),
            P(("rep", "tp")),
            P("tp", None, None),
        ),
        out_specs=P(("rep", "tp"), None, None),
        check_vma=False,
    )
```

```python
import functools
import math

import jax
import jax.numpy as jnp
from jax import lax
from jax.experimental import pallas as pl
from jax.experimental.pallas import tpu as pltpu
from jax.sharding import PartitionSpec as P

ROPE = 64
NOPE = 128
MESH = pl.DeviceIdType.MESH

ORDER = (8, 9, 7, 10, 6, 11, 5, 12, 4, 13, 3, 14, 2, 15, 1, 0)
PER_GROUP = 4
EARLY = (1, 0, 2, 3)
EARLY_PAIRS = (1,)


def kernel(
    n,
    lengths_hbm,
    rows_hbm,
    q_hbm,
    cache_hbm,
    new_hbm,
    up_hbm,
    out_ref,
    lengths_ref,
    rows_ref,
    new_ref,
    q_ref,
    cache_ref,
    up_ref,
    send1,
    recv1,
    send2,
    recv2,
    rows_out,
    rows_in,
    small_sem,
    load_sem,
    rows_send_sem,
    rows_recv_sem,
    send1_sem,
    recv1_sem,
    own1_sem,
    send2_sem,
    recv2_sem,
    own2_sem,
    ready_sem,
):
    rep = lax.axis_index("rep")
    me = lax.axis_index("tp")
    slots, drafts, _, heads = q_ref.shape
    ctx = cache_ref.shape[2]
    lat, values = up_hbm.shape[1], up_hbm.shape[2]
    own_heads = up_hbm.shape[0]
    pairs = drafts // 2
    groups = n // PER_GROUP
    per_block = slots * 2 * own_heads
    group_rows = PER_GROUP * per_block
    scale = (NOPE + ROPE) ** -0.5 * math.log2(math.e)

    loads = []
    for b in range(slots):
        loads.append(
            (
                pltpu.make_async_copy(cache_hbm.at[b], cache_ref.at[b], load_sem.at[2 * b]),
                pltpu.make_async_copy(q_hbm.at[b], q_ref.at[b], load_sem.at[2 * b + 1]),
            )
        )
    for copy in loads[0]:
        copy.start()

    core = me % 2
    barrier = pltpu.get_barrier_semaphore()

    def announce(semaphore, offsets):
        for k in offsets:
            pl.semaphore_signal(semaphore, inc=1, device_id=(rep, (me + k) % n), device_id_type=MESH)

    announce(barrier, [k for k in ORDER[:-1] if k % 2 == 0])

    @pl.when(core == 1)
    def _():
        announce(barrier, [k for k in ORDER if k % 2])

    small = []
    for i, (src, dst) in enumerate(((lengths_hbm, lengths_ref), (new_hbm, new_ref), (rows_hbm, rows_ref))):
        small.append(pltpu.make_async_copy(src, dst, small_sem.at[i]))
        small[-1].start()
    up_loads = []
    for h in range(own_heads):
        copy = pltpu.make_async_copy(
            up_hbm.at[h], up_ref.at[:, pl.ds(h * values, values)], load_sem.at[2 * slots + h]
        )
        up_loads.append(copy)

    chunks = lat // 128
    lines_slot = 2 * own_heads
    per_slot = lines_slot * chunks
    lane = lax.broadcasted_iota(jnp.int32, (1, 128), 1)
    for copy in small:
        copy.wait()
    rows_out[...] = jnp.where((lane // lines_slot) % 2 == 0, rows_ref[0], rows_ref[1])

    def attend(b, pair):
        q = jnp.concatenate([q_ref[b, 2 * pair], q_ref[b, 2 * pair + 1]], axis=1)
        keys = cache_ref[b]
        fresh = new_ref[b]
        old = lax.dot_general(q, keys, (((0,), (0,)), ((), ())), preferred_element_type=jnp.float32)
        new = lax.dot_general(q, fresh, (((0,), (1,)), ((), ())), preferred_element_type=jnp.float32)
        position = lax.broadcasted_iota(jnp.int32, (1, ctx), 1)
        old = jnp.where(position < lengths_ref[b], old, -jnp.inf)
        step = 2 * pair + lax.broadcasted_iota(jnp.int32, new.shape, 0) // heads
        new = jnp.where(lax.broadcasted_iota(jnp.int32, new.shape, 1) <= step, new, -jnp.inf)
        top = jnp.maximum(jnp.max(old, axis=1, keepdims=True), jnp.max(new, axis=1, keepdims=True))
        old = jnp.exp2((old - top) * scale)
        new = jnp.exp2((new - top) * scale)
        total = jnp.sum(old, axis=1, keepdims=True) + jnp.sum(new, axis=1, keepdims=True)
        mixed = lax.dot_general(
            old.astype(jnp.bfloat16), keys[:lat], (((1,), (1,)), ((), ())), preferred_element_type=jnp.float32
        )
        mixed = mixed + jnp.dot(new.astype(jnp.bfloat16), fresh[:, :lat], preferred_element_type=jnp.float32)
        latents = mixed * (1.0 / total)
        latents = latents.reshape(2, n, own_heads, lat)
        for d in range(n):
            block = jnp.concatenate([latents[0, d], latents[1, d]], axis=0).astype(jnp.bfloat16)
            for c in range(chunks):
                send1[pair, d, pl.ds(b * per_slot + c * lines_slot, lines_slot), :] = block[:, c * 128 : (c + 1) * 128]

    def send_first(pair, odd, first, last):
        part = pl.ds(first, last - first)
        for p, k in enumerate(ORDER):
            to = (me + k) % n
            if k % 2 != odd:
                continue
            if k == 0:
                if last == slots * per_slot:
                    pltpu.make_async_copy(send1.at[pair, me], recv1.at[pair, p], own1_sem.at[pair]).start()
                continue
            pltpu.make_async_remote_copy(
                src_ref=send1.at[pair, to, part],
                dst_ref=recv1.at[pair, p, part],
                send_sem=send1_sem.at[pair],
                recv_sem=recv1_sem.at[pair, p // PER_GROUP],
                device_id=(rep, to),
                device_id_type=MESH,
            ).start()

    def send_rows(odd):
        for p, k in enumerate(ORDER):
            if k and k % 2 == odd:
                pltpu.make_async_remote_copy(
                    src_ref=rows_out,
                    dst_ref=rows_in.at[p],
                    send_sem=rows_send_sem,
                    recv_sem=rows_recv_sem,
                    device_id=(rep, (me + k) % n),
                    device_id_type=MESH,
                ).start()

    def meet():
        pl.semaphore_wait(barrier, n // 2 - 1 + (n // 2) * (1 - core))

        @pl.when(core == 0)
        def _():
            announce(ready_sem, [k for k in ORDER if k % 2])

    pl.when(me == 0)(meet)
    for pair in range(pairs):
        for b in range(slots):
            if pair == 0:
                for copy in loads[b]:
                    copy.wait()
                if b == 0:
                    for copy in [*loads[1], *up_loads]:
                        copy.start()
            attend(b, pair)
            if pair == 0 and b == 0:
                pl.when(me != 0)(meet)

            if pair == 0:
                first, last = b * per_slot, (b + 1) * per_slot
            elif b == slots - 1:
                first, last = 0, slots * per_slot
            else:
                continue
            send_first(pair, 0, first, last)

            @pl.when(core == 0)
            def _():
                send_first(pair, 1, first, last)

            if pair == 0 and b == 0:
                send_rows(0)

                @pl.when(core == 0)
                def _():
                    send_rows(1)

    @pl.when(core == 1)
    def _():
        pl.semaphore_wait(ready_sem, n // 2)
        for pair in range(pairs):
            send_first(pair, 1, 0, slots * per_slot)
            if pair == 0:
                send_rows(1)

    for copy in up_loads:
        copy.wait()

    out_lines = n * 16
    o = lax.broadcasted_iota(jnp.int32, (out_lines, group_rows), 0)
    i = lax.broadcasted_iota(jnp.int32, (out_lines, group_rows), 1)
    want = (o // 16) * 2 + (o // 2) % 2
    same_draft = (o % 2) == (i // own_heads) % 2
    source = lax.broadcasted_iota(jnp.int32, (1, group_rows), 1) // per_block
    picks = []
    pltpu.make_async_copy(rows_in.at[pl.ds(0, n - 1)], rows_in.at[pl.ds(0, n - 1)], rows_recv_sem).wait()
    rows_in[n - 1] = rows_out[...]

    def pick(g):
        held = rows_in[g * PER_GROUP]
        for s in range(1, PER_GROUP):
            held = jnp.where(source == s, rows_in[g * PER_GROUP + s], held)
        return jnp.where((want == held) & same_draft, 1.0, 0.0).astype(jnp.bfloat16)

    line_head = lax.broadcasted_iota(jnp.int32, (group_rows, values), 0) % own_heads
    quarter = (lax.broadcasted_iota(jnp.int32, (out_lines, 256), 0) // 4) % 4

    for pair in range(pairs):
        ordered = None
        for g in range(groups):
            first = g * PER_GROUP
            count = min(PER_GROUP, n - 1 - first)
            arrived = recv1.at[pair, pl.ds(first, count)]
            pltpu.make_async_copy(arrived, arrived, recv1_sem.at[pair, g]).wait()
            if count < PER_GROUP:
                pltpu.make_async_copy(send1.at[pair, me], recv1.at[pair, n - 1], own1_sem.at[pair]).wait()
            if pair == 0:
                picks.append(pick(g))
            block = recv1[pair, pl.ds(first, PER_GROUP)]
            block = block.reshape(PER_GROUP * slots, chunks, lines_slot, 128)
            block = jnp.concatenate([block[:, c] for c in range(chunks)], axis=2).reshape(group_rows, lat)
            full = jnp.dot(block, up_ref[...], preferred_element_type=jnp.float32)
            kept = jnp.concatenate(
                [
                    jnp.where(line_head == h, full[:, h * values : (h + 1) * values], 0.0).astype(jnp.bfloat16)
                    for h in range(own_heads)
                ],
                axis=1,
            )
            part = jnp.dot(picks[g], kept, preferred_element_type=jnp.float32)
            ordered = part if ordered is None else ordered + part
        block = ordered[:, :256]
        for s in range(1, 4):
            block = jnp.where(quarter == s, ordered[:, s * 256 : (s + 1) * 256], block)
        send2[pair] = block.astype(jnp.bfloat16).reshape(n, 16, 256)
        columns = pl.ds(pl.multiple_of(me * 256, 256), 256)
        landing = recv2.at[pl.ds(pair * 16, 16), columns]
        pltpu.make_async_copy(send2.at[pair, me], landing, own2_sem.at[pair]).start()

        def send_second(to):
            pltpu.make_async_remote_copy(
                src_ref=send2.at[pair, to],
                dst_ref=landing,
                send_sem=send2_sem.at[pair],
                recv_sem=recv2_sem.at[pair],
                device_id=(rep, to),
                device_id_type=MESH,
            ).start()

        ahead = EARLY if pair in EARLY_PAIRS else ()
        for to in ahead:
            pl.when(me != to)(functools.partial(send_second, to))
        for k in ORDER[:-1]:
            to = (me + k) % n
            if ahead:
                pl.when(to >= len(ahead))(functools.partial(send_second, to))
            else:
                send_second(to)

    for pair in range(pairs):
        arrived = recv2.at[pl.ds(pair * 16, 16), pl.ds(0, (n - 1) * 256)]
        pltpu.make_async_copy(arrived, arrived, recv2_sem.at[pair]).wait()
        own = recv2.at[pl.ds(pair * 16, 16), pl.ds(pl.multiple_of(me * 256, 256), 256)]
        pltpu.make_async_copy(send2.at[pair, me], own, own2_sem.at[pair]).wait()

    lines = 4 * slots * drafts
    o = lax.broadcasted_iota(jnp.int32, (lines, pairs * 16), 0)
    i = lax.broadcasted_iota(jnp.int32, (lines, pairs * 16), 1)
    wanted = ((o % 4) // 2) * 16 + (o // 8) * 4 + ((o // 4) % 2) * 2 + o % 2
    place = jnp.where(i == wanted, 1.0, 0.0).astype(jnp.bfloat16)
    final = jnp.dot(place, recv2[...], preferred_element_type=jnp.float32)
    for s in range(n):
        for t in range(4):
            lines = final[t * 8 : (t + 1) * 8, s * 256 : (s + 1) * 256].astype(jnp.bfloat16)
            out_ref[:, :, pl.ds(s * 1024 + t * 256, 256)] = lines.reshape(slots, drafts, 256)

    pltpu.make_async_copy(rows_in.at[pl.ds(0, n - 1)], rows_in.at[pl.ds(0, n - 1)], rows_send_sem).wait()
    for pair in range(pairs):
        sent = send1.at[pair, pl.ds(0, n - 1)]
        pltpu.make_async_copy(sent, sent, send1_sem.at[pair]).wait()
        sent = send2.at[pair, pl.ds(0, n - 1)]
        pltpu.make_async_copy(sent, sent, send2_sem.at[pair]).wait()


def per_device(n, queries, latent_cache, new_latent, cached_lengths, slot_rows, up_weight):
    slots, drafts, heads, embed = queries.shape
    own_heads, lat, values = up_weight.shape
    ctx = latent_cache.shape[1]
    pairs = drafts // 2
    per_block = slots * 2 * own_heads
    vmem = pl.BlockSpec(memory_space=pltpu.VMEM)
    hbm = pl.BlockSpec(memory_space=pl.ANY)
    dma = pltpu.SemaphoreType.DMA
    bf16 = jnp.bfloat16
    return pl.pallas_call(
        functools.partial(kernel, n),
        out_shape=pltpu.VMEM((slots, drafts, heads * values), bf16),
        in_specs=[hbm] * 6,
        out_specs=vmem,
        scratch_shapes=[
            pltpu.SMEM((slots,), jnp.int32),
            pltpu.SMEM((slots,), jnp.int32),
            pltpu.VMEM((slots, drafts, embed), bf16),
            pltpu.VMEM((slots, drafts, embed, heads), bf16),
            pltpu.VMEM((slots, embed, ctx), bf16),
            pltpu.VMEM((lat, own_heads * values), bf16),
            pltpu.VMEM((pairs, n, per_block * lat // 128, 128), bf16),
            pltpu.VMEM((pairs, n, per_block * lat // 128, 128), bf16),
            pltpu.VMEM((pairs, n, 16, 256), bf16),
            pltpu.VMEM((pairs * 16, n * 256), bf16),
            pltpu.VMEM((1, 128), jnp.int32),
            pltpu.VMEM((n, 1, 128), jnp.int32),
            dma((3,)),
            dma((2 * slots + own_heads,)),
            dma,
            dma,
            dma((pairs,)),
            dma((pairs, n // PER_GROUP)),
            dma((pairs,)),
            dma((pairs,)),
            dma((pairs,)),
            dma((pairs,)),
            pltpu.SemaphoreType.REGULAR,
        ],
        compiler_params=pltpu.CompilerParams(collective_id=0, has_side_effects=True, vmem_limit_bytes=60 << 20),
    )(cached_lengths, slot_rows, queries.swapaxes(2, 3), latent_cache.swapaxes(1, 2), new_latent, up_weight)


def solution(mesh):
    return jax.shard_map(
        functools.partial(per_device, mesh.shape["tp"]),
        mesh=mesh,
        in_specs=(
            P(("rep", "tp"), None, None, None),
            P(("rep", "tp"), None, None),
            P(("rep", "tp"), None, None),
            P(("rep", "tp")),
            P(("rep", "tp")),
            P("tp", None, None),
        ),
        out_specs=P(("rep", "tp"), None, None),
        check_vma=False,
    )
```

```python
import functools
import math

import jax
import jax.numpy as jnp
from jax import lax
from jax.experimental import pallas as pl
from jax.experimental.pallas import tpu as pltpu
from jax.sharding import PartitionSpec as P

ROPE = 64
NOPE = 128
MESH = pl.DeviceIdType.MESH

ORDER = (8, 9, 7, 10, 6, 11, 5, 12, 4, 13, 3, 14, 2, 15, 1, 0)
PER_GROUP = 4
EARLY = (1, 0, 2, 3)
EARLY_PAIRS = (1,)


def kernel(
    n,
    lengths_hbm,
    rows_hbm,
    q_hbm,
    cache_hbm,
    new_hbm,
    up_hbm,
    out_ref,
    lengths_ref,
    rows_ref,
    new_ref,
    q_ref,
    cache_ref,
    up_ref,
    send1,
    recv1,
    send2,
    recv2,
    rows_out,
    rows_in,
    small_sem,
    load_sem,
    rows_send_sem,
    rows_recv_sem,
    send1_sem,
    recv1_sem,
    own1_sem,
    send2_sem,
    recv2_sem,
    own2_sem,
    ready_sem,
):
    rep = lax.axis_index("rep")
    me = lax.axis_index("tp")
    slots, drafts, _, heads = q_ref.shape
    ctx = cache_ref.shape[2]
    lat, values = up_hbm.shape[1], up_hbm.shape[2]
    own_heads = up_hbm.shape[0]
    pairs = drafts // 2
    groups = n // PER_GROUP
    per_block = slots * 2 * own_heads
    group_rows = PER_GROUP * per_block
    scale = (NOPE + ROPE) ** -0.5 * math.log2(math.e)

    loads = []
    for b in range(slots):
        loads.append(
            (
                pltpu.make_async_copy(cache_hbm.at[b], cache_ref.at[b], load_sem.at[2 * b]),
                pltpu.make_async_copy(q_hbm.at[b], q_ref.at[b], load_sem.at[2 * b + 1]),
            )
        )
    for copy in loads[0]:
        copy.start()

    core = me % 2
    barrier = pltpu.get_barrier_semaphore()

    def announce(semaphore, offsets):
        for k in offsets:
            pl.semaphore_signal(semaphore, inc=1, device_id=(rep, (me + k) % n), device_id_type=MESH)

    announce(barrier, [k for k in ORDER[:-1] if k % 2 == 0])

    @pl.when(core == 1)
    def _():
        announce(barrier, [k for k in ORDER if k % 2])

    small = []
    for i, (src, dst) in enumerate(((lengths_hbm, lengths_ref), (new_hbm, new_ref), (rows_hbm, rows_ref))):
        small.append(pltpu.make_async_copy(src, dst, small_sem.at[i]))
        small[-1].start()
    up_loads = []
    for h in range(own_heads):
        copy = pltpu.make_async_copy(
            up_hbm.at[h], up_ref.at[:, pl.ds(h * values, values)], load_sem.at[2 * slots + h]
        )
        up_loads.append(copy)

    chunks = lat // 128
    lines_slot = 2 * own_heads
    per_slot = lines_slot * chunks
    lane = lax.broadcasted_iota(jnp.int32, (1, 128), 1)
    for copy in small:
        copy.wait()
    rows_out[...] = jnp.where((lane // lines_slot) % 2 == 0, rows_ref[0], rows_ref[1])

    def attend(b, pair):
        q = jnp.concatenate([q_ref[b, 2 * pair], q_ref[b, 2 * pair + 1]], axis=1)
        keys = cache_ref[b]
        fresh = new_ref[b]
        old = lax.dot_general(q, keys, (((0,), (0,)), ((), ())), preferred_element_type=jnp.float32)
        new = lax.dot_general(q, fresh, (((0,), (1,)), ((), ())), preferred_element_type=jnp.float32)
        position = lax.broadcasted_iota(jnp.int32, (1, ctx), 1)
        old = jnp.where(position < lengths_ref[b], old, -jnp.inf)
        step = 2 * pair + lax.broadcasted_iota(jnp.int32, new.shape, 0) // heads
        new = jnp.where(lax.broadcasted_iota(jnp.int32, new.shape, 1) <= step, new, -jnp.inf)
        top = jnp.maximum(jnp.max(old, axis=1, keepdims=True), jnp.max(new, axis=1, keepdims=True))
        old = jnp.exp2((old - top) * scale)
        new = jnp.exp2((new - top) * scale)
        total = jnp.sum(old, axis=1, keepdims=True) + jnp.sum(new, axis=1, keepdims=True)
        mixed = lax.dot_general(
            old.astype(jnp.bfloat16), keys[:lat], (((1,), (1,)), ((), ())), preferred_element_type=jnp.float32
        )
        mixed = mixed + jnp.dot(new.astype(jnp.bfloat16), fresh[:, :lat], preferred_element_type=jnp.float32)
        latents = mixed * (1.0 / total)
        latents = latents.reshape(2, n, own_heads, lat)
        for d in range(n):
            block = jnp.concatenate([latents[0, d], latents[1, d]], axis=0).astype(jnp.bfloat16)
            for c in range(chunks):
                send1[pair, d, pl.ds(b * per_slot + c * lines_slot, lines_slot), :] = block[:, c * 128 : (c + 1) * 128]

    def send_first(pair, odd, first, last):
        part = pl.ds(first, last - first)
        for p, k in enumerate(ORDER):
            to = (me + k) % n
            if k % 2 != odd:
                continue
            if k == 0:
                if last == slots * per_slot:
                    pltpu.make_async_copy(send1.at[pair, me], recv1.at[pair, p], own1_sem.at[pair]).start()
                continue
            pltpu.make_async_remote_copy(
                src_ref=send1.at[pair, to, part],
                dst_ref=recv1.at[pair, p, part],
                send_sem=send1_sem.at[pair],
                recv_sem=recv1_sem.at[pair, p // PER_GROUP],
                device_id=(rep, to),
                device_id_type=MESH,
            ).start()

    def send_rows(odd):
        for p, k in enumerate(ORDER):
            if k and k % 2 == odd:
                pltpu.make_async_remote_copy(
                    src_ref=rows_out,
                    dst_ref=rows_in.at[p],
                    send_sem=rows_send_sem,
                    recv_sem=rows_recv_sem,
                    device_id=(rep, (me + k) % n),
                    device_id_type=MESH,
                ).start()

    def meet():
        pl.semaphore_wait(barrier, n // 2 - 1 + (n // 2) * (1 - core))

        @pl.when(core == 0)
        def _():
            announce(ready_sem, [k for k in ORDER if k % 2])

    pl.when(me == 0)(meet)
    for pair in range(pairs):
        for b in range(slots):
            if pair == 0:
                for copy in loads[b]:
                    copy.wait()
                if b == 0:
                    for copy in [*loads[1], *up_loads]:
                        copy.start()
            attend(b, pair)
            if pair == 0 and b == 0:
                pl.when(me != 0)(meet)

            if pair == 0:
                first, last = b * per_slot, (b + 1) * per_slot
            elif b == slots - 1:
                first, last = 0, slots * per_slot
            else:
                continue
            send_first(pair, 0, first, last)

            @pl.when(core == 0)
            def _():
                send_first(pair, 1, first, last)

            if pair == 0 and b == slots - 1:
                send_rows(0)

                @pl.when(core == 0)
                def _():
                    send_rows(1)

    @pl.when(core == 1)
    def _():
        pl.semaphore_wait(ready_sem, n // 2)
        for pair in range(pairs):
            send_first(pair, 1, 0, slots * per_slot)
            if pair == 0:
                send_rows(1)

    for copy in up_loads:
        copy.wait()

    out_lines = n * 16
    o = lax.broadcasted_iota(jnp.int32, (out_lines, group_rows), 0)
    i = lax.broadcasted_iota(jnp.int32, (out_lines, group_rows), 1)
    want = (o // 16) * 2 + (o // 2) % 2
    same_draft = (o % 2) == (i // own_heads) % 2
    source = lax.broadcasted_iota(jnp.int32, (1, group_rows), 1) // per_block
    picks = []
    pltpu.make_async_copy(rows_in.at[pl.ds(0, n - 1)], rows_in.at[pl.ds(0, n - 1)], rows_recv_sem).wait()
    rows_in[n - 1] = rows_out[...]

    def pick(g):
        held = rows_in[g * PER_GROUP]
        for s in range(1, PER_GROUP):
            held = jnp.where(source == s, rows_in[g * PER_GROUP + s], held)
        return jnp.where((want == held) & same_draft, 1.0, 0.0).astype(jnp.bfloat16)

    line_head = lax.broadcasted_iota(jnp.int32, (group_rows, values), 0) % own_heads
    quarter = (lax.broadcasted_iota(jnp.int32, (out_lines, 256), 0) // 4) % 4

    for pair in range(pairs):
        ordered = None
        for g in range(groups):
            first = g * PER_GROUP
            count = min(PER_GROUP, n - 1 - first)
            arrived = recv1.at[pair, pl.ds(first, count)]
            pltpu.make_async_copy(arrived, arrived, recv1_sem.at[pair, g]).wait()
            if count < PER_GROUP:
                pltpu.make_async_copy(send1.at[pair, me], recv1.at[pair, n - 1], own1_sem.at[pair]).wait()
            if pair == 0:
                picks.append(pick(g))
            block = recv1[pair, pl.ds(first, PER_GROUP)]
            block = block.reshape(PER_GROUP * slots, chunks, lines_slot, 128)
            block = jnp.concatenate([block[:, c] for c in range(chunks)], axis=2).reshape(group_rows, lat)
            full = jnp.dot(block, up_ref[...], preferred_element_type=jnp.float32)
            kept = jnp.concatenate(
                [
                    jnp.where(line_head == h, full[:, h * values : (h + 1) * values], 0.0).astype(jnp.bfloat16)
                    for h in range(own_heads)
                ],
                axis=1,
            )
            part = jnp.dot(picks[g], kept, preferred_element_type=jnp.float32)
            ordered = part if ordered is None else ordered + part
        block = ordered[:, :256]
        for s in range(1, 4):
            block = jnp.where(quarter == s, ordered[:, s * 256 : (s + 1) * 256], block)
        send2[pair] = block.astype(jnp.bfloat16).reshape(n, 16, 256)
        columns = pl.ds(pl.multiple_of(me * 256, 256), 256)
        landing = recv2.at[pl.ds(pair * 16, 16), columns]
        pltpu.make_async_copy(send2.at[pair, me], landing, own2_sem.at[pair]).start()

        def send_second(to):
            pltpu.make_async_remote_copy(
                src_ref=send2.at[pair, to],
                dst_ref=landing,
                send_sem=send2_sem.at[pair],
                recv_sem=recv2_sem.at[pair],
                device_id=(rep, to),
                device_id_type=MESH,
            ).start()

        ahead = EARLY if pair in EARLY_PAIRS else ()
        for to in ahead:
            pl.when(me != to)(functools.partial(send_second, to))
        for k in ORDER[:-1]:
            to = (me + k) % n
            if ahead:
                pl.when(to >= len(ahead))(functools.partial(send_second, to))
            else:
                send_second(to)

    for pair in range(pairs):
        arrived = recv2.at[pl.ds(pair * 16, 16), pl.ds(0, (n - 1) * 256)]
        pltpu.make_async_copy(arrived, arrived, recv2_sem.at[pair]).wait()
        own = recv2.at[pl.ds(pair * 16, 16), pl.ds(pl.multiple_of(me * 256, 256), 256)]
        pltpu.make_async_copy(send2.at[pair, me], own, own2_sem.at[pair]).wait()

    lines = 4 * slots * drafts
    o = lax.broadcasted_iota(jnp.int32, (lines, pairs * 16), 0)
    i = lax.broadcasted_iota(jnp.int32, (lines, pairs * 16), 1)
    wanted = ((o % 4) // 2) * 16 + (o // 8) * 4 + ((o // 4) % 2) * 2 + o % 2
    place = jnp.where(i == wanted, 1.0, 0.0).astype(jnp.bfloat16)
    final = jnp.dot(place, recv2[...], preferred_element_type=jnp.float32)
    for s in range(n):
        for t in range(4):
            lines = final[t * 8 : (t + 1) * 8, s * 256 : (s + 1) * 256].astype(jnp.bfloat16)
            out_ref[:, :, pl.ds(s * 1024 + t * 256, 256)] = lines.reshape(slots, drafts, 256)

    pltpu.make_async_copy(rows_in.at[pl.ds(0, n - 1)], rows_in.at[pl.ds(0, n - 1)], rows_send_sem).wait()
    for pair in range(pairs):
        sent = send1.at[pair, pl.ds(0, n - 1)]
        pltpu.make_async_copy(sent, sent, send1_sem.at[pair]).wait()
        sent = send2.at[pair, pl.ds(0, n - 1)]
        pltpu.make_async_copy(sent, sent, send2_sem.at[pair]).wait()


def per_device(n, queries, latent_cache, new_latent, cached_lengths, slot_rows, up_weight):
    slots, drafts, heads, embed = queries.shape
    own_heads, lat, values = up_weight.shape
    ctx = latent_cache.shape[1]
    pairs = drafts // 2
    per_block = slots * 2 * own_heads
    vmem = pl.BlockSpec(memory_space=pltpu.VMEM)
    hbm = pl.BlockSpec(memory_space=pl.ANY)
    dma = pltpu.SemaphoreType.DMA
    bf16 = jnp.bfloat16
    return pl.pallas_call(
        functools.partial(kernel, n),
        out_shape=pltpu.VMEM((slots, drafts, heads * values), bf16),
        in_specs=[hbm] * 6,
        out_specs=vmem,
        scratch_shapes=[
            pltpu.SMEM((slots,), jnp.int32),
            pltpu.SMEM((slots,), jnp.int32),
            pltpu.VMEM((slots, drafts, embed), bf16),
            pltpu.VMEM((slots, drafts, embed, heads), bf16),
            pltpu.VMEM((slots, embed, ctx), bf16),
            pltpu.VMEM((lat, own_heads * values), bf16),
            pltpu.VMEM((pairs, n, per_block * lat // 128, 128), bf16),
            pltpu.VMEM((pairs, n, per_block * lat // 128, 128), bf16),
            pltpu.VMEM((pairs, n, 16, 256), bf16),
            pltpu.VMEM((pairs * 16, n * 256), bf16),
            pltpu.VMEM((1, 128), jnp.int32),
            pltpu.VMEM((n, 1, 128), jnp.int32),
            dma((3,)),
            dma((2 * slots + own_heads,)),
            dma,
            dma,
            dma((pairs,)),
            dma((pairs, n // PER_GROUP)),
            dma((pairs,)),
            dma((pairs,)),
            dma((pairs,)),
            dma((pairs,)),
            pltpu.SemaphoreType.REGULAR,
        ],
        compiler_params=pltpu.CompilerParams(collective_id=0, has_side_effects=True, vmem_limit_bytes=60 << 20),
    )(cached_lengths, slot_rows, queries.swapaxes(2, 3), latent_cache.swapaxes(1, 2), new_latent, up_weight)


def solution(mesh):
    return jax.shard_map(
        functools.partial(per_device, mesh.shape["tp"]),
        mesh=mesh,
        in_specs=(
            P(("rep", "tp"), None, None, None),
            P(("rep", "tp"), None, None),
            P(("rep", "tp"), None, None),
            P(("rep", "tp")),
            P(("rep", "tp")),
            P("tp", None, None),
        ),
        out_specs=P(("rep", "tp"), None, None),
        check_vma=False,
    )
```
